1024 devices in a mesh: inter: 16 (over x_hi, y), intra: 64 (over x_lo, z, core).
Axes of the slice: x: 4 (x_hi: 2, x_lo: 2; x = x_hi * 2 + x_lo), y: 8, z: 16, core: 2. Of those that a mesh axis runs over, the one named last changes fastest.
Arguments:
- tokens: bfloat16 [131072, 4096], P(('inter', 'intra')), may hold values from -6 to 6
- key_grad: bfloat16 [131072, 512], P(('inter', 'intra')), may hold values from -6 to 6
- codes: bfloat16 [4096, 512], P(('intra', 'inter')), may hold values from -6 to 6
- scales: bfloat16 [4096, 4], P(('intra', 'inter')), may hold values from 0.0039978027 to 0.039794922
Outputs:
- keys: bfloat16 [131072, 512], P(('inter', 'intra'))
- input_grad: bfloat16 [131072, 4096], P(('inter', 'intra'))
- weight_grad: float32 [4096, 512], P(('intra', 'inter'))
The draws below stay inside these ranges and needn't reach their ends.
All inputs are finite; a program needn't handle non-finite values.
Results may differ from the reference program's by a relative error of at most 0.0049.
Values may be sent and summed in bfloat16 or wider, within the bound.
No kernel may reach another device: no remote copies, remote signals or barrier semaphores. Data moves between devices by JAX's collectives and lax.ppermute only.
A program may use at most 128 MiB of HBM per device.

```python
import math
import jax
import jax.numpy as jnp
from jax import lax

D_IN = 4096
KV = 512
BLOCK = 128
TOK_DEV = 128
TOKENS = 131072
N_INTER = 16
N_INTRA = 64


def steps_of(own_key, shape, split, smallest, top_value):
    factor_of = 1.0
    for dim, blocks in split:
        heights = jax.random.uniform(jax.random.fold_in(jax.random.fold_in(own_key, 6), dim), (blocks,), jnp.float32, smallest / len(split), top_value / len(split))
        factor_of = factor_of * jnp.repeat(jnp.exp(heights), shape[dim] // blocks).reshape((-1,) + (1,) * (len(shape) - 1 - dim))
    return factor_of


def normal_values(rng, dims, spread, most, split=(), dtype=jnp.bfloat16):
    entries = spread * jax.random.normal(rng, dims, jnp.float32)
    if split:
        entries = entries * steps_of(rng, dims, split, -0.22, 0.18)
    return jnp.clip(entries, -most, most).astype(dtype)


def setup_inputs(seed: int = 0) -> dict:
    splits = jax.random.split(jax.random.key(seed), 5)
    return {
        "tokens": normal_values(splits[0], (TOKENS, D_IN), 1.0, 6.0, ((0, 1024),)),
        "key_grad": normal_values(splits[1], (TOKENS, KV), 1.0, 6.0, ((0, 1024),)),
        "codes": normal_values(splits[2], (D_IN, KV), 1.0, 6.0, ((0, 1024),)),
        "scales": jnp.clip(jnp.exp(math.log(0.039794922) - 2.2979944 * jax.random.uniform(splits[3], (D_IN, KV // BLOCK), jnp.float32) ** steps_of(splits[3], (D_IN, KV // BLOCK), ((0, 1024),), -0.2, 0.2)), 0.0039978027, 0.039794922).astype(jnp.bfloat16),
    }


def dequantize(codes, scales):
    rows = codes.shape[0]
    blocks = codes.astype(jnp.float32).reshape(rows, KV // BLOCK, BLOCK)
    scaled = blocks * scales.astype(jnp.float32)[:, :, None]
    return scaled.reshape(rows, KV).astype(jnp.bfloat16)


def reference(tokens, key_grad, codes, scales):
    weight = dequantize(codes, scales)
    keys = jnp.dot(tokens, weight, preferred_element_type=jnp.float32).astype(jnp.bfloat16)
    input_grad = jnp.dot(key_grad, weight.T, preferred_element_type=jnp.float32).astype(jnp.bfloat16)
    count = N_INTER * N_INTRA
    tok_blocks = tokens.reshape(count, TOK_DEV, D_IN)
    grad_blocks = key_grad.reshape(count, TOK_DEV, KV)

    def add_device(total, pair):
        rows, grads = pair
        partial_value = jnp.dot(rows.T, grads, preferred_element_type=jnp.float32)
        rounded = partial_value.astype(jnp.bfloat16)
        rounded = lax.optimization_barrier(rounded)
        return total + rounded.astype(jnp.float32), None

    weight_grad, _ = lax.scan(add_device, jnp.zeros((D_IN, KV), jnp.float32), (tok_blocks, grad_blocks))
    return keys, input_grad, weight_grad
```

```python
import jax
import jax.numpy as jnp
from jax import lax
from jax.sharding import Mesh, PartitionSpec as P

KV = 512
BLOCK = 128
D_IN = 4096
INTER = ("xh", "y")
INTRA = ("xl", "z", "c")
SIZES = (2, 8, 2, 16, 2)
F32 = jnp.float32
BF16 = jnp.bfloat16


def dequantize(codes, scales):
    rows = codes.shape[0]
    blocks = codes.astype(F32).reshape(rows, KV // BLOCK, BLOCK)
    scaled = blocks * scales.astype(F32)[:, :, None]
    return scaled.reshape(rows, KV).astype(BF16)


def exchange(blocks, axis):
    return lax.all_to_all(blocks, axis, split_axis=0, concat_axis=0, tiled=True)


def gather_weight(part):
    by_z = exchange(jnp.broadcast_to(part[None], (16, 4, KV)), "z").reshape(64, KV)
    by_y = exchange(jnp.broadcast_to(by_z[None], (8, 64, KV)), "y")
    rows = by_y.reshape(8, 16, 4, KV).transpose(1, 0, 2, 3).reshape(512, KV)
    by_x = exchange(jnp.broadcast_to(rows[None], (4, 512, KV)), ("xh", "xl"))
    own = by_x.reshape(2048, KV)
    other = lax.ppermute(own, "c", [(0, 1), (1, 0)])
    first = lax.axis_index("c") == 0
    both = jnp.stack([jnp.where(first, own, other), jnp.where(first, other, own)])
    both = both.reshape(2, 2, 2, 16, 32, KV).transpose(2, 3, 0, 1, 4, 5)
    return both.reshape(D_IN, KV)


def scatter_sum(partial):
    blocks = partial.reshape(2, 16, 2, 2, 32, KV).transpose(2, 3, 0, 1, 4, 5)
    by_c = exchange(blocks.reshape(2, 2048, KV), "c")
    total = (by_c[0].astype(F32) + by_c[1].astype(F32)).astype(BF16)
    by_x = exchange(total.reshape(4, 512, KV), ("xh", "xl"))
    total = jnp.sum(by_x.astype(F32), axis=0).astype(BF16)
    total = total.reshape(16, 8, 4, KV).transpose(1, 0, 2, 3).reshape(8, 64, KV)
    by_y = exchange(total, "y")
    total = jnp.sum(by_y.astype(F32), axis=0).astype(BF16)
    by_z = exchange(total.reshape(16, 4, KV), "z")
    return jnp.sum(by_z.astype(F32), axis=0)


def shards(tokens, key_grad, codes, scales):
    part = dequantize(codes, scales)
    partial = lax.dot_general(
        tokens, key_grad, (((0,), (0,)), ((), ())), preferred_element_type=F32
    ).astype(BF16)
    weight_grad = scatter_sum(partial)
    weight = gather_weight(part)
    keys = jnp.dot(tokens, weight, preferred_element_type=F32).astype(BF16)
    input_grad = lax.dot_general(
        key_grad, weight, (((1,), (1,)), ((), ())), preferred_element_type=F32
    ).astype(BF16)
    return keys, input_grad, weight_grad


def solution(mesh):
    torus = Mesh(mesh.devices.reshape(SIZES), ("xh", "y", "xl", "z", "c"))
    tokens_over = P(INTER + INTRA, None)
    rows_over = P(INTRA + INTER, None)
    return jax.shard_map(
        shards,
        mesh=torus,
        in_specs=(tokens_over, tokens_over, rows_over, rows_over),
        out_specs=(tokens_over, tokens_over, rows_over),
        check_vma=False,
    )
```

```python
import jax
import jax.numpy as jnp
from jax import lax
from jax.experimental import pallas as pl
from jax.experimental.pallas import tpu as pltpu
from jax.sharding import Mesh, PartitionSpec as P

KV = 512
BLOCK = 128
TOK = 128
NY = 8
NZ = 16
ROWS = 4
HALF = NZ * NY * ROWS
SLICE = 2 * HALF
PAY = SLICE + KV
INTER = ("xh", "y")
INTRA = ("xl", "z", "c")
F32 = jnp.float32
BF16 = jnp.bfloat16
INTERPRET = False
SWAP = [(0, 1), (1, 0)]
NN = (((1,), (0,)), ((), ()))
NT = (((1,), (1,)), ((), ()))
TN = (((0,), (0,)), ((), ()))


def dot(a, b, dims):
    return lax.dot_general(a, b, dims, preferred_element_type=F32)


def iota(shape, dim):
    return lax.broadcasted_iota(jnp.int32, shape, dim)


def one_hot(hit):
    return jnp.where(hit, 1.0, 0.0).astype(BF16)


def x_split(xh):
    row, lane = iota((128, 128), 0), iota((128, 128), 1)
    c, q = (row >> 5) & 1, row & 31
    half = jnp.where(row < 64, xh, 1 - xh)
    return one_hot(lane == c * 64 + half * 32 + q)


def y_outer():
    row, col = iota((HALF, HALF), 0), iota((HALF, HALF), 1)
    r = row & (ROWS - 1)
    z = (row >> 2) & (NZ - 1)
    y = row // (NZ * ROWS)
    return one_hot(col == z * (NY * ROWS) + y * ROWS + r)


def eye():
    return one_hot(iota((128, 128), 0) == iota((128, 128), 1))


def prepare(tok_ref, grad_ref, *outs):
    xh, xl = lax.axis_index("xh"), lax.axis_index("xl")
    split = x_split(xh)
    for kl in range(2):
        col = (xl if kl == 0 else 1 - xl) * (NZ * 128)
        for z in range(NZ):
            block = tok_ref[:, pl.ds(pl.multiple_of(col + z * 128, 128), 128)]
            piece = dot(split, block, NT).astype(BF16)
            for kh in range(2):
                for c in range(2):
                    at = kh * 64 + c * 32
                    outs[2 * kh + kl][pl.ds(c * HALF + z * 32, 32), :] = piece[at : at + 32]
    same = eye()
    for b in range(KV // 128):
        piece = dot(same, grad_ref[:, b * 128 : (b + 1) * 128], NT).astype(BF16)
        for out in outs:
            out[pl.ds(SLICE + b * 128, 128), :] = piece


def partial_sums(r0, r1, r2, r3, keep, send):
    c = lax.axis_index("c")
    refs = (r0, r1, r2, r3)
    grads = jnp.concatenate([r[SLICE:, :] for r in refs], axis=1)
    for out, half in ((send, 1 - c), (keep, c)):
        at = pl.ds(pl.multiple_of(half * HALF, HALF), HALF)
        rows = jnp.concatenate([r[at, :] for r in refs], axis=1)
        out[...] = dot(rows, grads, NT).astype(BF16)


def add_cores(a, b, out):
    total = (a[...].astype(F32) + b[...].astype(F32)).astype(BF16)
    out[...] = dot(y_outer(), total, NN).astype(BF16)


def apply_weight(own, other, r0, r1, r2, r3, o0, o1, o2, o3, weight):
    c = lax.axis_index("c")
    refs, outs = (r0, r1, r2, r3), (o0, o1, o2, o3)
    order = y_outer()
    for ref, half in ((own, c), (other, 1 - c)):
        at = pl.ds(pl.multiple_of(half * HALF, HALF), HALF)
        weight[at, :] = dot(order, ref[...], TN).astype(BF16)
    w = weight[...]
    grads = jnp.concatenate([r[SLICE:, :] for r in refs], axis=1)
    back = dot(w, grads, NN).astype(BF16)
    for k, out in enumerate(outs):
        out[:SLICE, :] = back[:, k * TOK : (k + 1) * TOK]
    rows = jnp.concatenate([r[:SLICE, :] for r in refs], axis=1)
    keys = dot(w, rows, TN).astype(BF16)
    for k, out in enumerate(outs):
        out[SLICE:, :] = keys[:, k * TOK : (k + 1) * TOK]


def finish(f0, f1, f2, f3, keys, input_grad):
    xh, xl = lax.axis_index("xh"), lax.axis_index("xl")
    refs = (f0, f1, f2, f3)
    same, split = eye(), x_split(xh)
    for b in range(KV // 128):
        at = pl.ds(SLICE + b * 128, 128)
        total = sum(r[at, :].astype(F32) for r in refs).astype(BF16)
        keys[:, b * 128 : (b + 1) * 128] = dot(total, same, TN).astype(BF16)
    for kl in range(2):
        col = (xl if kl == 0 else 1 - xl) * (NZ * 128)
        for z in range(NZ):
            piece = jnp.concatenate(
                [
                    refs[2 * kh + kl][pl.ds(c * HALF + z * 32, 32), :]
                    for kh in range(2)
                    for c in range(2)
                ],
                axis=0,
            )
            block = dot(piece, split, TN).astype(BF16)
            input_grad[:, pl.ds(pl.multiple_of(col + z * 128, 128), 128)] = block


def kernel(body, outs, flops, moved, scratch=()):
    return pl.pallas_call(
        body,
        out_shape=[jax.ShapeDtypeStruct(s, BF16) for s in outs],
        scratch_shapes=list(scratch),
        compiler_params=pltpu.CompilerParams(vmem_limit_bytes=24 * 1024 * 1024),
        cost_estimate=pl.CostEstimate(flops=flops, bytes_accessed=moved, transcendentals=0),
        interpret=INTERPRET,
    )


def dequantize(codes, scales):
    rows = codes.shape[0]
    blocks = codes.astype(F32).reshape(rows, KV // BLOCK, BLOCK)
    scaled = blocks * scales.astype(F32)[:, :, None]
    return scaled.reshape(rows, KV).astype(BF16)


def exchange(blocks, axis):
    return lax.all_to_all(blocks, axis, split_axis=0, concat_axis=0, tiled=True)


def to_members(blocks):
    return (
        blocks[0],
        lax.ppermute(blocks[1], "xl", SWAP),
        lax.ppermute(blocks[2], "xh", SWAP),
        lax.ppermute(blocks[3], ("xh", "xl"), [(0, 3), (1, 2), (2, 1), (3, 0)]),
    )


def shards(tokens, key_grad, codes, scales):
    part = dequantize(codes, scales)
    blocks = kernel(prepare, [(PAY, TOK)] * 4, 1 << 28, 3 << 20)(tokens, key_grad)
    work = to_members(blocks)
    by_z = exchange(jnp.broadcast_to(part[None], (NZ, ROWS, KV)), "z")
    by_z = by_z.reshape(NZ * ROWS, KV)
    by_y = exchange(jnp.broadcast_to(by_z[None], (NY, NZ * ROWS, KV)), "y")
    own = by_y.reshape(HALF, KV)
    other = lax.ppermute(own, "c", SWAP)
    keep, send = kernel(partial_sums, [(HALF, KV)] * 2, 1 << 29, 3 << 20)(*work)
    got = lax.ppermute(send, "c", SWAP)
    (total,) = kernel(add_cores, [(HALF, KV)], 1 << 28, 3 << 19)(keep, got)
    total = exchange(total.reshape(NY, NZ * ROWS, KV), "y")
    total = jnp.sum(total.astype(F32), axis=0).astype(BF16)
    total = exchange(total.reshape(NZ, ROWS, KV), "z")
    weight_grad = jnp.sum(total.astype(F32), axis=0)
    results = kernel(
        apply_weight, [(PAY, TOK)] * 4, 1 << 30, 4 << 20, [pltpu.VMEM((SLICE, KV), BF16)]
    )(own, other, *work)
    results = to_members(results)
    d_in = 4 * SLICE
    keys, input_grad = kernel(finish, [(TOK, KV), (TOK, d_in)], 1 << 28, 3 << 20)(*results)
    return keys, input_grad, weight_grad


def solution(mesh):
    torus = Mesh(mesh.devices.reshape(2, NY, 2, NZ, 2), ("xh", "y", "xl", "z", "c"))
    tokens_over = P(INTER + INTRA, None)
    rows_over = P(INTRA + INTER, None)
    return jax.shard_map(
        shards,
        mesh=torus,
        in_specs=(tokens_over, tokens_over, rows_over, rows_over),
        out_specs=(tokens_over, tokens_over, rows_over),
        check_vma=False,
    )
```

```python
import jax
import jax.numpy as jnp
from jax import lax
from jax.experimental import pallas as pl
from jax.experimental.pallas import tpu as pltpu
from jax.sharding import Mesh, PartitionSpec as P

KV = 512
BLOCK = 128
TOK = 128
NY = 8
NZ = 16
ROWS = 4
HALF = NZ * NY * ROWS
SLICE = 2 * HALF
PAY = SLICE + KV
INTER = ("xh", "y")
INTRA = ("xl", "z", "c")
F32 = jnp.float32
BF16 = jnp.bfloat16
INTERPRET = False
SWAP = [(0, 1), (1, 0)]
NN = (((1,), (0,)), ((), ()))
NT = (((1,), (1,)), ((), ()))
TN = (((0,), (0,)), ((), ()))


def dot(a, b, dims):
    return lax.dot_general(a, b, dims, preferred_element_type=F32)


def iota(shape, dim):
    return lax.broadcasted_iota(jnp.int32, shape, dim)


def one_hot(hit):
    return jnp.where(hit, 1.0, 0.0).astype(BF16)


def x_split(xh):
    row, lane = iota((128, 128), 0), iota((128, 128), 1)
    c, q = (row >> 5) & 1, row & 31
    half = jnp.where(row < 64, xh, 1 - xh)
    return one_hot(lane == c * 64 + half * 32 + q)


def y_outer():
    row, col = iota((HALF, HALF), 0), iota((HALF, HALF), 1)
    r = row & (ROWS - 1)
    z = (row >> 2) & (NZ - 1)
    y = row // (NZ * ROWS)
    return one_hot(col == z * (NY * ROWS) + y * ROWS + r)


def eye():
    return one_hot(iota((128, 128), 0) == iota((128, 128), 1))


def prepare(tok_ref, grad_ref, *outs):
    xh, xl = lax.axis_index("xh"), lax.axis_index("xl")
    split = x_split(xh)
    for kl in range(2):
        col = (xl if kl == 0 else 1 - xl) * (NZ * 128)
        for z in range(NZ):
            block = tok_ref[:, pl.ds(pl.multiple_of(col + z * 128, 128), 128)]
            piece = dot(split, block, NT).astype(BF16)
            for kh in range(2):
                for c in range(2):
                    at = kh * 64 + c * 32
                    outs[2 * kh + kl][pl.ds(c * HALF + z * 32, 32), :] = piece[at : at + 32]
    same = eye()
    for b in range(KV // 128):
        piece = dot(same, grad_ref[:, b * 128 : (b + 1) * 128], NT).astype(BF16)
        for out in outs:
            out[pl.ds(SLICE + b * 128, 128), :] = piece


def scale_rows(codes, scales, later, copies):
    del later
    for b in range(KV // BLOCK):
        at = slice(b * BLOCK, (b + 1) * BLOCK)
        scaled = codes[:, at].astype(F32) * scales[:, b : b + 1].astype(F32)
        copies[:, :, at] = jnp.broadcast_to(scaled.astype(BF16)[None], (NZ, ROWS, BLOCK))


def partial_sums(r0, r1, r2, r3, keep, send):
    c = lax.axis_index("c")
    refs = (r0, r1, r2, r3)
    grads = jnp.concatenate([r[SLICE:, :] for r in refs], axis=1)
    for out, half in ((send, 1 - c), (keep, c)):
        at = pl.ds(pl.multiple_of(half * HALF, HALF), HALF)
        rows = jnp.concatenate([r[at, :] for r in refs], axis=1)
        out[...] = dot(rows, grads, NT).astype(BF16)


def add_cores(a, b, out):
    total = (a[...].astype(F32) + b[...].astype(F32)).astype(BF16)
    out[...] = dot(y_outer(), total, NN).astype(BF16)


def apply_weight(own, other, r0, r1, r2, r3, o0, o1, o2, o3, weight):
    c = lax.axis_index("c")
    refs, outs = (r0, r1, r2, r3), (o0, o1, o2, o3)
    order = y_outer()
    for ref, half in ((own, c), (other, 1 - c)):
        at = pl.ds(pl.multiple_of(half * HALF, HALF), HALF)
        weight[at, :] = dot(order, ref[...], TN).astype(BF16)
    w = weight[...]
    grads = jnp.concatenate([r[SLICE:, :] for r in refs], axis=1)
    back = dot(w, grads, NN).astype(BF16)
    for k, out in enumerate(outs):
        out[:SLICE, :] = back[:, k * TOK : (k + 1) * TOK]
    rows = jnp.concatenate([r[:SLICE, :] for r in refs], axis=1)
    keys = dot(w, rows, TN).astype(BF16)
    for k, out in enumerate(outs):
        out[SLICE:, :] = keys[:, k * TOK : (k + 1) * TOK]


def finish(f0, f1, f2, f3, keys, input_grad):
    xh, xl = lax.axis_index("xh"), lax.axis_index("xl")
    refs = (f0, f1, f2, f3)
    same, split = eye(), x_split(xh)
    for b in range(KV // 128):
        at = pl.ds(SLICE + b * 128, 128)
        total = sum(r[at, :].astype(F32) for r in refs).astype(BF16)
        keys[:, b * 128 : (b + 1) * 128] = dot(total, same, TN).astype(BF16)
    for kl in range(2):
        col = (xl if kl == 0 else 1 - xl) * (NZ * 128)
        for z in range(NZ):
            piece = jnp.concatenate(
                [
                    refs[2 * kh + kl][pl.ds(c * HALF + z * 32, 32), :]
                    for kh in range(2)
                    for c in range(2)
                ],
                axis=0,
            )
            block = dot(piece, split, TN).astype(BF16)
            input_grad[:, pl.ds(pl.multiple_of(col + z * 128, 128), 128)] = block


def kernel(body, outs, flops, moved, scratch=(), any_of=None):
    specs = {}
    if any_of is not None:
        whole = [pl.BlockSpec(memory_space=pltpu.VMEM)] * any_of
        specs = {"in_specs": [*whole, pl.BlockSpec(memory_space=pl.ANY)]}
    return pl.pallas_call(
        body,
        **specs,
        out_shape=[jax.ShapeDtypeStruct(s, BF16) for s in outs],
        scratch_shapes=list(scratch),
        compiler_params=pltpu.CompilerParams(vmem_limit_bytes=24 * 1024 * 1024),
        cost_estimate=pl.CostEstimate(flops=flops, bytes_accessed=moved, transcendentals=0),
        interpret=INTERPRET,
    )


def exchange(blocks, axis):
    return lax.all_to_all(blocks, axis, split_axis=0, concat_axis=0, tiled=True)


def to_members(blocks):
    return (
        blocks[0],
        lax.ppermute(blocks[1], "xl", SWAP),
        lax.ppermute(blocks[2], "xh", SWAP),
        lax.ppermute(blocks[3], ("xh", "xl"), [(0, 3), (1, 2), (2, 1), (3, 0)]),
    )


def shards(tokens, key_grad, codes, scales):
    blocks = kernel(prepare, [(PAY, TOK)] * 4, 1 << 28, 3 << 20)(tokens, key_grad)
    work = to_members(blocks)
    (copies,) = kernel(scale_rows, [(NZ, ROWS, KV)], 1 << 12, 1 << 17, any_of=2)(
        codes, scales, blocks[0]
    )
    by_z = exchange(copies, "z")
    by_z, one, two = lax.optimization_barrier((by_z, work[1], work[2]))
    work = (work[0], one, two, work[3])
    by_z = by_z.reshape(NZ * ROWS, KV)
    by_y = exchange(jnp.broadcast_to(by_z[None], (NY, NZ * ROWS, KV)), "y")
    own = by_y.reshape(HALF, KV)
    other = lax.ppermute(own, "c", SWAP)
    keep, send = kernel(partial_sums, [(HALF, KV)] * 2, 1 << 29, 3 << 20)(*work)
    got = lax.ppermute(send, "c", SWAP)
    (total,) = kernel(add_cores, [(HALF, KV)], 1 << 28, 3 << 19)(keep, got)
    total = exchange(total.reshape(NY, NZ * ROWS, KV), "y")
    total = jnp.sum(total.astype(F32), axis=0).astype(BF16)
    total = exchange(total.reshape(NZ, ROWS, KV), "z")
    weight_grad = jnp.sum(total.astype(F32), axis=0)
    results = kernel(
        apply_weight, [(PAY, TOK)] * 4, 1 << 30, 4 << 20, [pltpu.VMEM((SLICE, KV), BF16)]
    )(own, other, *work)
    results = to_members(results)
    d_in = 4 * SLICE
    keys, input_grad = kernel(finish, [(TOK, KV), (TOK, d_in)], 1 << 28, 3 << 20)(*results)
    return keys, input_grad, weight_grad


def solution(mesh):
    torus = Mesh(mesh.devices.reshape(2, NY, 2, NZ, 2), ("xh", "y", "xl", "z", "c"))
    tokens_over = P(INTER + INTRA, None)
    rows_over = P(INTRA + INTER, None)
    return jax.shard_map(
        shards,
        mesh=torus,
        in_specs=(tokens_over, tokens_over, rows_over, rows_over),
        out_specs=(tokens_over, tokens_over, rows_over),
        check_vma=False,
    )
```

```python
import jax
import jax.numpy as jnp
from jax import lax
from jax.experimental import pallas as pl
from jax.experimental.pallas import tpu as pltpu
from jax.sharding import Mesh, PartitionSpec as P

KV = 512
BLOCK = 128
TOK = 128
NY = 8
NZ = 16
ROWS = 4
HALF = NZ * NY * ROWS
SLICE = 2 * HALF
PAY = SLICE + KV
INTER = ("xh", "y")
INTRA = ("xl", "z", "c")
F32 = jnp.float32
BF16 = jnp.bfloat16
INTERPRET = False
SWAP = [(0, 1), (1, 0)]
NN = (((1,), (0,)), ((), ()))
NT = (((1,), (1,)), ((), ()))
TN = (((0,), (0,)), ((), ()))


def dot(a, b, dims):
    return lax.dot_general(a, b, dims, preferred_element_type=F32)


def iota(shape, dim):
    return lax.broadcasted_iota(jnp.int32, shape, dim)


def one_hot(hit):
    return jnp.where(hit, 1.0, 0.0).astype(BF16)


def x_split(xh):
    row, lane = iota((128, 128), 0), iota((128, 128), 1)
    c, q = (row >> 5) & 1, row & 31
    half = jnp.where(row < 64, xh, 1 - xh)
    return one_hot(lane == c * 64 + half * 32 + q)


def y_outer():
    row, col = iota((HALF, HALF), 0), iota((HALF, HALF), 1)
    r = row & (ROWS - 1)
    z = (row >> 2) & (NZ - 1)
    y = row // (NZ * ROWS)
    return one_hot(col == z * (NY * ROWS) + y * ROWS + r)


def eye():
    return one_hot(iota((128, 128), 0) == iota((128, 128), 1))


def prepare(tok_ref, grad_ref, *refs):
    outs, (tok, grad, sems) = refs[:4], refs[4:]
    xh, xl = lax.axis_index("xh"), lax.axis_index("xl")
    wide = NZ * 128 // 2
    copies = [pltpu.make_async_copy(grad_ref, grad, sems.at[4])]
    for i in range(4):
        col = (xl if i < 2 else 1 - xl) * (NZ * 128) + (i % 2) * wide
        there = tok_ref.at[:, pl.ds(pl.multiple_of(col, 128), wide)]
        copies.append(pltpu.make_async_copy(there, tok.at[i], sems.at[i]))
    for copy in copies:
        copy.start()
    same, split = eye(), x_split(xh)
    copies[0].wait()
    for b in range(KV // 128):
        piece = dot(same, grad[:, b * 128 : (b + 1) * 128], NT).astype(BF16)
        for out in outs:
            out[pl.ds(SLICE + b * 128, 128), :] = piece
    for i in range(4):
        copies[1 + i].wait()
        for j in range(NZ // 2):
            z = (i % 2) * (NZ // 2) + j
            piece = dot(split, tok[i, :, j * 128 : (j + 1) * 128], NT).astype(BF16)
            for kh in range(2):
                for c in range(2):
                    at = kh * 64 + c * 32
                    outs[2 * kh + i // 2][pl.ds(c * HALF + z * 32, 32), :] = piece[at : at + 32]


def scale_rows(codes, scales, copies):
    for b in range(KV // BLOCK):
        at = slice(b * BLOCK, (b + 1) * BLOCK)
        scaled = codes[:, at].astype(F32) * scales[:, b : b + 1].astype(F32)
        copies[:, :, at] = jnp.broadcast_to(scaled.astype(BF16)[None], (NZ, ROWS, BLOCK))


def partial_sums(r0, r1, r2, r3, keep, send):
    c = lax.axis_index("c")
    refs = (r0, r1, r2, r3)
    grads = jnp.concatenate([r[SLICE:, :] for r in refs], axis=1)
    for out, half in ((send, 1 - c), (keep, c)):
        at = pl.ds(pl.multiple_of(half * HALF, HALF), HALF)
        rows = jnp.concatenate([r[at, :] for r in refs], axis=1)
        out[...] = dot(rows, grads, NT).astype(BF16)


def add_cores(a, b, out):
    total = (a[...].astype(F32) + b[...].astype(F32)).astype(BF16)
    out[...] = dot(y_outer(), total, NN).astype(BF16)


def apply_weight(own, other, r0, r1, r2, r3, o0, o1, o2, o3, weight):
    c = lax.axis_index("c")
    refs, outs = (r0, r1, r2, r3), (o0, o1, o2, o3)
    order = y_outer()
    for ref, half in ((own, c), (other, 1 - c)):
        at = pl.ds(pl.multiple_of(half * HALF, HALF), HALF)
        weight[at, :] = dot(order, ref[...], TN).astype(BF16)
    w = weight[...]
    grads = jnp.concatenate([r[SLICE:, :] for r in refs], axis=1)
    back = dot(w, grads, NN).astype(BF16)
    for k, out in enumerate(outs):
        out[:SLICE, :] = back[:, k * TOK : (k + 1) * TOK]
    rows = jnp.concatenate([r[:SLICE, :] for r in refs], axis=1)
    keys = dot(w, rows, TN).astype(BF16)
    for k, out in enumerate(outs):
        out[SLICE:, :] = keys[:, k * TOK : (k + 1) * TOK]


def finish(f0, f1, f2, f3, keys, input_grad):
    xh, xl = lax.axis_index("xh"), lax.axis_index("xl")
    refs = (f0, f1, f2, f3)
    same, split = eye(), x_split(xh)
    for b in range(KV // 128):
        at = pl.ds(SLICE + b * 128, 128)
        total = sum(r[at, :].astype(F32) for r in refs).astype(BF16)
        keys[:, b * 128 : (b + 1) * 128] = dot(total, same, TN).astype(BF16)
    for kl in range(2):
        col = (xl if kl == 0 else 1 - xl) * (NZ * 128)
        for z in range(NZ):
            piece = jnp.concatenate(
                [
                    refs[2 * kh + kl][pl.ds(c * HALF + z * 32, 32), :]
                    for kh in range(2)
                    for c in range(2)
                ],
                axis=0,
            )
            block = dot(piece, split, TN).astype(BF16)
            input_grad[:, pl.ds(pl.multiple_of(col + z * 128, 128), 128)] = block


def last_sum(blocks, out):
    out[...] = jnp.sum(blocks[...].astype(F32), axis=0)


def kernel(body, outs, flops, moved, scratch=(), in_hbm=0, vmem=24, dtype=BF16):
    return pl.pallas_call(
        body,
        **({"in_specs": [pl.BlockSpec(memory_space=pl.ANY)] * in_hbm} if in_hbm else {}),
        out_shape=[jax.ShapeDtypeStruct(s, dtype) for s in outs],
        scratch_shapes=list(scratch),
        compiler_params=pltpu.CompilerParams(vmem_limit_bytes=vmem << 20),
        cost_estimate=pl.CostEstimate(flops=flops, bytes_accessed=moved, transcendentals=0),
        interpret=INTERPRET,
    )


def exchange(blocks, axis):
    return lax.all_to_all(blocks, axis, split_axis=0, concat_axis=0, tiled=True)


def far(block):
    return lax.ppermute(block, "xh", SWAP)


def near(block):
    return lax.ppermute(block, "xl", SWAP)


def next_to(block):
    return lax.ppermute(block, ("xh", "xl"), [(0, 3), (1, 2), (2, 1), (3, 0)])


def shards(tokens, key_grad, codes, scales):
    (copies,) = kernel(scale_rows, [(NZ, ROWS, KV)], 1 << 12, 1 << 17)(codes, scales)
    room = [
        pltpu.VMEM((4, TOK, NZ * 64), BF16),
        pltpu.VMEM((TOK, KV), BF16),
        pltpu.SemaphoreType.DMA((5,)),
    ]
    blocks = kernel(prepare, [(PAY, TOK)] * 4, 1 << 28, 3 << 20, room, 2, 60)(tokens, key_grad)
    work = far(blocks[2]), near(blocks[1]), next_to(blocks[3])
    work = blocks[0], work[1], work[0], work[2]
    by_z = exchange(copies, "z").reshape(NZ * ROWS, KV)
    by_y = exchange(jnp.broadcast_to(by_z[None], (NY, NZ * ROWS, KV)), "y")
    own = by_y.reshape(HALF, KV)
    other = lax.ppermute(own, "c", SWAP)
    keep, send = kernel(partial_sums, [(HALF, KV)] * 2, 1 << 29, 3 << 20)(*work)
    got = lax.ppermute(send, "c", SWAP)
    (total,) = kernel(add_cores, [(HALF, KV)], 1 << 28, 3 << 19)(keep, got)
    total = exchange(total.reshape(NY, NZ * ROWS, KV), "y")
    total = jnp.sum(total.astype(F32), axis=0).astype(BF16)
    results = kernel(
        apply_weight, [(PAY, TOK)] * 4, 1 << 30, 4 << 20, [pltpu.VMEM((SLICE, KV), BF16)]
    )(own, other, *work)
    from_far = far(results[2])
    total, one, three = lax.optimization_barrier((total, results[1], results[3]))
    total = exchange(total.reshape(NZ, ROWS, KV), "z")
    total, from_far = lax.optimization_barrier((total, from_far))
    results = results[0], near(one), from_far, next_to(three)
    (weight_grad,) = kernel(last_sum, [(ROWS, KV)], 1 << 36, 1 << 17, dtype=F32)(total)
    d_in = 4 * SLICE
    keys, input_grad = kernel(finish, [(TOK, KV), (TOK, d_in)], 1 << 28, 3 << 20)(*results)
    return keys, input_grad, weight_grad


def solution(mesh):
    torus = Mesh(mesh.devices.reshape(2, NY, 2, NZ, 2), ("xh", "y", "xl", "z", "c"))
    tokens_over = P(INTER + INTRA, None)
    rows_over = P(INTRA + INTER, None)
    return jax.shard_map(
        shards,
        mesh=torus,
        in_specs=(tokens_over, tokens_over, rows_over, rows_over),
        out_specs=(tokens_over, tokens_over, rows_over),
        check_vma=False,
    )
```

```python
import jax
import jax.numpy as jnp
from jax import lax
from jax.experimental import pallas as pl
from jax.experimental.pallas import tpu as pltpu
from jax.sharding import Mesh, PartitionSpec as P

KV = 512
BLOCK = 128
TOK = 128
NY = 8
NZ = 16
ROWS = 4
HALF = NZ * NY * ROWS
SLICE = 2 * HALF
PAY = SLICE + KV
INTER = ("xh", "y")
INTRA = ("xl", "z", "c")
F32 = jnp.float32
BF16 = jnp.bfloat16
INTERPRET = False
SWAP = [(0, 1), (1, 0)]
NN = (((1,), (0,)), ((), ()))
NT = (((1,), (1,)), ((), ()))
TN = (((0,), (0,)), ((), ()))


def dot(a, b, dims):
    return lax.dot_general(a, b, dims, preferred_element_type=F32)


def iota(shape, dim):
    return lax.broadcasted_iota(jnp.int32, shape, dim)


def one_hot(hit):
    return jnp.where(hit, 1.0, 0.0).astype(BF16)


def x_split(xh):
    row, lane = iota((128, 128), 0), iota((128, 128), 1)
    c, q = (row >> 5) & 1, row & 31
    half = jnp.where(row < 64, xh, 1 - xh)
    return one_hot(lane == c * 64 + half * 32 + q)


def y_outer():
    row, col = iota((HALF, HALF), 0), iota((HALF, HALF), 1)
    r = row & (ROWS - 1)
    z = (row >> 2) & (NZ - 1)
    y = row // (NZ * ROWS)
    return one_hot(col == z * (NY * ROWS) + y * ROWS + r)


def eye():
    return one_hot(iota((128, 128), 0) == iota((128, 128), 1))


def prepare(tok_ref, grad_ref, *outs):
    xh, xl = lax.axis_index("xh"), lax.axis_index("xl")
    split = x_split(xh)
    for kl in range(2):
        col = (xl if kl == 0 else 1 - xl) * (NZ * 128)
        for z in range(NZ):
            block = tok_ref[:, pl.ds(pl.multiple_of(col + z * 128, 128), 128)]
            piece = dot(split, block, NT).astype(BF16)
            for kh in range(2):
                for c in range(2):
                    at = kh * 64 + c * 32
                    outs[2 * kh + kl][pl.ds(c * HALF + z * 32, 32), :] = piece[at : at + 32]
    same = eye()
    for b in range(KV // 128):
        piece = dot(same, grad_ref[:, b * 128 : (b + 1) * 128], NT).astype(BF16)
        for out in outs:
            out[pl.ds(SLICE + b * 128, 128), :] = piece


def scale_rows(codes, scales, copies):
    for b in range(KV // BLOCK):
        at = slice(b * BLOCK, (b + 1) * BLOCK)
        scaled = codes[:, at].astype(F32) * scales[:, b : b + 1].astype(F32)
        copies[:, :, at] = jnp.broadcast_to(scaled.astype(BF16)[None], (NZ, ROWS, BLOCK))


def partial_sums(r0, r2, r1, r3, keep, send):
    c = lax.axis_index("c")
    refs = (r0, r1, r2, r3)
    grads = jnp.concatenate([r[SLICE:, :] for r in refs], axis=1)
    for out, half in ((send, 1 - c), (keep, c)):
        at = pl.ds(pl.multiple_of(half * HALF, HALF), HALF)
        rows = jnp.concatenate([r[at, :] for r in refs], axis=1)
        out[...] = dot(rows, grads, NT).astype(BF16)


def add_cores(a, b, out):
    total = (a[...].astype(F32) + b[...].astype(F32)).astype(BF16)
    out[...] = dot(y_outer(), total, NN).astype(BF16)


def apply_weight(own, other, r0, r1, r2, r3, o0, o1, o2, o3, weight):
    c = lax.axis_index("c")
    refs, outs = (r0, r1, r2, r3), (o0, o1, o2, o3)
    order = y_outer()
    for ref, half in ((own, c), (other, 1 - c)):
        at = pl.ds(pl.multiple_of(half * HALF, HALF), HALF)
        weight[at, :] = dot(order, ref[...], TN).astype(BF16)
    w = weight[...]
    grads = jnp.concatenate([r[SLICE:, :] for r in refs], axis=1)
    back = dot(w, grads, NN).astype(BF16)
    for k, out in enumerate(outs):
        out[:SLICE, :] = back[:, k * TOK : (k + 1) * TOK]
    rows = jnp.concatenate([r[:SLICE, :] for r in refs], axis=1)
    keys = dot(w, rows, TN).astype(BF16)
    for k, out in enumerate(outs):
        out[SLICE:, :] = keys[:, k * TOK : (k + 1) * TOK]


def finish(f0, f2, f1, f3, keys, input_grad):
    xh, xl = lax.axis_index("xh"), lax.axis_index("xl")
    refs = (f0, f1, f2, f3)
    same, split = eye(), x_split(xh)
    for b in range(KV // 128):
        at = pl.ds(SLICE + b * 128, 128)
        total = sum(r[at, :].astype(F32) for r in refs).astype(BF16)
        keys[:, b * 128 : (b + 1) * 128] = dot(total, same, TN).astype(BF16)
    for kl in range(2):
        col = (xl if kl == 0 else 1 - xl) * (NZ * 128)
        for z in range(NZ):
            piece = jnp.concatenate(
                [
                    refs[2 * kh + kl][pl.ds(c * HALF + z * 32, 32), :]
                    for kh in range(2)
                    for c in range(2)
                ],
                axis=0,
            )
            block = dot(piece, split, TN).astype(BF16)
            input_grad[:, pl.ds(pl.multiple_of(col + z * 128, 128), 128)] = block


def kernel(body, outs, flops, moved, scratch=()):
    return pl.pallas_call(
        body,
        out_shape=[jax.ShapeDtypeStruct(s, BF16) for s in outs],
        scratch_shapes=list(scratch),
        compiler_params=pltpu.CompilerParams(vmem_limit_bytes=24 * 1024 * 1024),
        cost_estimate=pl.CostEstimate(flops=flops, bytes_accessed=moved, transcendentals=0),
        interpret=INTERPRET,
    )


def exchange(blocks, axis):
    return lax.all_to_all(blocks, axis, split_axis=0, concat_axis=0, tiled=True)


def far_first(blocks):
    return [blocks[k] for k in (0, 2, 1, 3)]


def to_members(blocks):
    return (
        blocks[0],
        lax.ppermute(blocks[1], "xl", SWAP),
        lax.ppermute(blocks[2], "xh", SWAP),
        lax.ppermute(blocks[3], ("xh", "xl"), [(0, 3), (1, 2), (2, 1), (3, 0)]),
    )


def shards(tokens, key_grad, codes, scales):
    blocks = kernel(prepare, [(PAY, TOK)] * 4, 1 << 28, 3 << 20)(tokens, key_grad)
    work = to_members(blocks)
    (copies,) = kernel(scale_rows, [(NZ, ROWS, KV)], 1 << 12, 1 << 17)(codes, scales)
    by_z = exchange(copies, "z")
    by_z, two = lax.optimization_barrier((by_z, work[2]))
    work = (work[0], work[1], two, work[3])
    by_z = by_z.reshape(NZ * ROWS, KV)
    by_y = exchange(jnp.broadcast_to(by_z[None], (NY, NZ * ROWS, KV)), "y")
    own = by_y.reshape(HALF, KV)
    other = lax.ppermute(own, "c", SWAP)
    keep, send = kernel(partial_sums, [(HALF, KV)] * 2, 1 << 29, 3 << 20)(*far_first(work))
    got = lax.ppermute(send, "c", SWAP)
    (total,) = kernel(add_cores, [(HALF, KV)], 1 << 28, 3 << 19)(keep, got)
    total = exchange(total.reshape(NY, NZ * ROWS, KV), "y")
    total = jnp.sum(total.astype(F32), axis=0).astype(BF16)
    total = exchange(total.reshape(NZ, ROWS, KV), "z")
    weight_grad = jnp.sum(total.astype(F32), axis=0)
    results = kernel(
        apply_weight, [(PAY, TOK)] * 4, 1 << 30, 4 << 20, [pltpu.VMEM((SLICE, KV), BF16)]
    )(own, other, *work)
    results = to_members(results)
    d_in = 4 * SLICE
    keys, input_grad = kernel(finish, [(TOK, KV), (TOK, d_in)], 1 << 28, 3 << 20)(*far_first(results))
    return keys, input_grad, weight_grad


def solution(mesh):
    torus = Mesh(mesh.devices.reshape(2, NY, 2, NZ, 2), ("xh", "y", "xl", "z", "c"))
    tokens_over = P(INTER + INTRA, None)
    rows_over = P(INTRA + INTER, None)
    return jax.shard_map(
        shards,
        mesh=torus,
        in_specs=(tokens_over, tokens_over, rows_over, rows_over),
        out_specs=(tokens_over, tokens_over, rows_over),
        check_vma=False,
    )
```

```python
import jax
import jax.numpy as jnp
from jax import lax
from jax.experimental import pallas as pl
from jax.experimental.pallas import tpu as pltpu
from jax.sharding import Mesh, PartitionSpec as P

KV = 512
BLOCK = 128
TOK = 128
NY = 8
NZ = 16
ROWS = 4
HALF = NZ * NY * ROWS
SLICE = 2 * HALF
PAY = SLICE + KV
INTER = ("xh", "y")
INTRA = ("xl", "z", "c")
F32 = jnp.float32
BF16 = jnp.bfloat16
INTERPRET = False
SWAP = [(0, 1), (1, 0)]
NN = (((1,), (0,)), ((), ()))
NT = (((1,), (1,)), ((), ()))
TN = (((0,), (0,)), ((), ()))


def dot(a, b, dims):
    return lax.dot_general(a, b, dims, preferred_element_type=F32)


def iota(shape, dim):
    return lax.broadcasted_iota(jnp.int32, shape, dim)


def one_hot(hit):
    return jnp.where(hit, 1.0, 0.0).astype(BF16)


def x_split(xh):
    row, lane = iota((128, 128), 0), iota((128, 128), 1)
    c, q = (row >> 5) & 1, row & 31
    half = jnp.where(row < 64, xh, 1 - xh)
    return one_hot(lane == c * 64 + half * 32 + q)


def y_outer():
    row, col = iota((HALF, HALF), 0), iota((HALF, HALF), 1)
    r = row & (ROWS - 1)
    z = (row >> 2) & (NZ - 1)
    y = row // (NZ * ROWS)
    return one_hot(col == z * (NY * ROWS) + y * ROWS + r)


def eye():
    return one_hot(iota((128, 128), 0) == iota((128, 128), 1))


def prepare(tok_ref, grad_ref, *outs):
    xh, xl = lax.axis_index("xh"), lax.axis_index("xl")
    split = x_split(xh)
    for kl in range(2):
        col = (xl if kl == 0 else 1 - xl) * (NZ * 128)
        for z in range(NZ):
            block = tok_ref[:, pl.ds(pl.multiple_of(col + z * 128, 128), 128)]
            piece = dot(split, block, NT).astype(BF16)
            for kh in range(2):
                for c in range(2):
                    at = kh * 64 + c * 32
                    outs[2 * kh + kl][pl.ds(c * HALF + z * 32, 32), :] = piece[at : at + 32]
    same = eye()
    for b in range(KV // 128):
        piece = dot(same, grad_ref[:, b * 128 : (b + 1) * 128], NT).astype(BF16)
        for out in outs:
            out[pl.ds(SLICE + b * 128, 128), :] = piece


def scale_rows(codes_ref, scales_ref, copies, codes, scales, sems):
    loads = [
        pltpu.make_async_copy(codes_ref, codes, sems.at[0]),
        pltpu.make_async_copy(scales_ref, scales, sems.at[1]),
    ]
    for load in loads:
        load.start()
    for load in loads:
        load.wait()
    for b in range(KV // BLOCK):
        at = slice(b * BLOCK, (b + 1) * BLOCK)
        scaled = codes[:, at].astype(F32) * scales[:, b : b + 1].astype(F32)
        copies[:, :, at] = jnp.broadcast_to(scaled.astype(BF16)[None], (NZ, ROWS, BLOCK))


def partial_sums(r0, r2, r1, r3, keep, send):
    c = lax.axis_index("c")
    refs = (r0, r1, r2, r3)
    grads = jnp.concatenate([r[SLICE:, :] for r in refs], axis=1)
    for out, half in ((send, 1 - c), (keep, c)):
        at = pl.ds(pl.multiple_of(half * HALF, HALF), HALF)
        rows = jnp.concatenate([r[at, :] for r in refs], axis=1)
        out[...] = dot(rows, grads, NT).astype(BF16)


def add_cores(a, b, out):
    total = (a[...].astype(F32) + b[...].astype(F32)).astype(BF16)
    out[...] = dot(y_outer(), total, NN).astype(BF16)


def apply_weight(own, other, r0, r1, r2, r3, o0, o1, o2, o3, weight):
    c = lax.axis_index("c")
    refs, outs = (r0, r1, r2, r3), (o0, o1, o2, o3)
    order = y_outer()
    for ref, half in ((own, c), (other, 1 - c)):
        at = pl.ds(pl.multiple_of(half * HALF, HALF), HALF)
        weight[at, :] = dot(order, ref[...], TN).astype(BF16)
    w = weight[...]
    grads = jnp.concatenate([r[SLICE:, :] for r in refs], axis=1)
    back = dot(w, grads, NN).astype(BF16)
    for k, out in enumerate(outs):
        out[:SLICE, :] = back[:, k * TOK : (k + 1) * TOK]
    rows = jnp.concatenate([r[:SLICE, :] for r in refs], axis=1)
    keys = dot(w, rows, TN).astype(BF16)
    for k, out in enumerate(outs):
        out[SLICE:, :] = keys[:, k * TOK : (k + 1) * TOK]


def finish(f0, f2, f1, f3, keys, input_grad):
    xh, xl = lax.axis_index("xh"), lax.axis_index("xl")
    refs = (f0, f1, f2, f3)
    same, split = eye(), x_split(xh)
    for b in range(KV // 128):
        at = pl.ds(SLICE + b * 128, 128)
        total = sum(r[at, :].astype(F32) for r in refs).astype(BF16)
        keys[:, b * 128 : (b + 1) * 128] = dot(total, same, TN).astype(BF16)
    for kl in range(2):
        col = (xl if kl == 0 else 1 - xl) * (NZ * 128)
        for z in range(NZ):
            piece = jnp.concatenate(
                [
                    refs[2 * kh + kl][pl.ds(c * HALF + z * 32, 32), :]
                    for kh in range(2)
                    for c in range(2)
                ],
                axis=0,
            )
            block = dot(piece, split, TN).astype(BF16)
            input_grad[:, pl.ds(pl.multiple_of(col + z * 128, 128), 128)] = block


def kernel(body, outs, flops, moved, scratch=(), in_hbm=0, vmem=24):
    pinned = [pl.BlockSpec(memory_space=pl.ANY)] * in_hbm
    return pl.pallas_call(
        body,
        **({"in_specs": pinned} if in_hbm else {}),
        out_shape=[jax.ShapeDtypeStruct(s, BF16) for s in outs],
        scratch_shapes=list(scratch),
        compiler_params=pltpu.CompilerParams(vmem_limit_bytes=vmem << 20),
        cost_estimate=pl.CostEstimate(flops=flops, bytes_accessed=moved, transcendentals=0),
        interpret=INTERPRET,
    )


def exchange(blocks, axis):
    return lax.all_to_all(blocks, axis, split_axis=0, concat_axis=0, tiled=True)


def far_first(blocks):
    return [blocks[k] for k in (0, 2, 1, 3)]


def to_members(blocks):
    return (
        blocks[0],
        lax.ppermute(blocks[1], "xl", SWAP),
        lax.ppermute(blocks[2], "xh", SWAP),
        lax.ppermute(blocks[3], ("xh", "xl"), [(0, 3), (1, 2), (2, 1), (3, 0)]),
    )


def shards(tokens, key_grad, codes, scales):
    room = [
        pltpu.VMEM((ROWS, KV), BF16),
        pltpu.VMEM((ROWS, KV // BLOCK), BF16),
        pltpu.SemaphoreType.DMA((2,)),
    ]
    (copies,) = kernel(scale_rows, [(NZ, ROWS, KV)], 1 << 12, 1 << 17, room, 2, 60)(codes, scales)
    blocks = kernel(prepare, [(PAY, TOK)] * 4, 1 << 28, 3 << 20)(tokens, key_grad)
    work = to_members(blocks)
    by_z = exchange(copies, "z")
    by_z = by_z.reshape(NZ * ROWS, KV)
    by_y = exchange(jnp.broadcast_to(by_z[None], (NY, NZ * ROWS, KV)), "y")
    keep, send = kernel(partial_sums, [(HALF, KV)] * 2, 1 << 29, 3 << 20)(*far_first(work))
    got = lax.ppermute(send, "c", SWAP)
    (total,) = kernel(add_cores, [(HALF, KV)], 1 << 28, 3 << 19)(keep, got)
    by_y, total = lax.optimization_barrier((by_y, total))
    own = by_y.reshape(HALF, KV)
    other = lax.ppermute(own, "c", SWAP)
    total = exchange(total.reshape(NY, NZ * ROWS, KV), "y")
    total = jnp.sum(total.astype(F32), axis=0).astype(BF16)
    total = exchange(total.reshape(NZ, ROWS, KV), "z")
    results = kernel(
        apply_weight, [(PAY, TOK)] * 4, 1 << 30, 4 << 20, [pltpu.VMEM((SLICE, KV), BF16)]
    )(own, other, *work)
    results = to_members(results)
    d_in = 4 * SLICE
    keys, input_grad = kernel(finish, [(TOK, KV), (TOK, d_in)], 1 << 31, 3 << 20)(
        *far_first(results)
    )
    total, keys, input_grad = lax.optimization_barrier((total, keys, input_grad))
    weight_grad = jnp.sum(total.astype(F32), axis=0)
    return keys, input_grad, weight_grad


def solution(mesh):
    torus = Mesh(mesh.devices.reshape(2, NY, 2, NZ, 2), ("xh", "y", "xl", "z", "c"))
    tokens_over = P(INTER + INTRA, None)
    rows_over = P(INTRA + INTER, None)
    return jax.shard_map(
        shards,
        mesh=torus,
        in_specs=(tokens_over, tokens_over, rows_over, rows_over),
        out_specs=(tokens_over, tokens_over, rows_over),
        check_vma=False,
    )
```

```python
import jax
import jax.numpy as jnp
from jax import lax
from jax.experimental import pallas as pl
from jax.experimental.pallas import tpu as pltpu
from jax.sharding import Mesh, PartitionSpec as P

KV = 512
BLOCK = 128
TOK = 128
NY = 8
NZ = 16
ROWS = 4
HALF = NZ * NY * ROWS
SLICE = 2 * HALF
PAY = SLICE + KV
INTER = ("xh", "y")
INTRA = ("xl", "z", "c")
F32 = jnp.float32
BF16 = jnp.bfloat16
INTERPRET = False
SWAP = [(0, 1), (1, 0)]
NN = (((1,), (0,)), ((), ()))
NT = (((1,), (1,)), ((), ()))
TN = (((0,), (0,)), ((), ()))


def dot(a, b, dims):
    return lax.dot_general(a, b, dims, preferred_element_type=F32)


def iota(shape, dim):
    return lax.broadcasted_iota(jnp.int32, shape, dim)


def one_hot(hit):
    return jnp.where(hit, 1.0, 0.0).astype(BF16)


def x_split(xh):
    row, lane = iota((128, 128), 0), iota((128, 128), 1)
    c, q = (row >> 5) & 1, row & 31
    half = jnp.where(row < 64, xh, 1 - xh)
    return one_hot(lane == c * 64 + half * 32 + q)


def y_outer():
    row, col = iota((HALF, HALF), 0), iota((HALF, HALF), 1)
    r = row & (ROWS - 1)
    z = (row >> 2) & (NZ - 1)
    y = row // (NZ * ROWS)
    return one_hot(col == z * (NY * ROWS) + y * ROWS + r)


def eye():
    return one_hot(iota((128, 128), 0) == iota((128, 128), 1))


def prepare(tok_ref, grad_ref, *outs):
    xh, xl = lax.axis_index("xh"), lax.axis_index("xl")
    split = x_split(xh)
    for kl in range(2):
        col = (xl if kl == 0 else 1 - xl) * (NZ * 128)
        for z in range(NZ):
            block = tok_ref[:, pl.ds(pl.multiple_of(col + z * 128, 128), 128)]
            piece = dot(split, block, NT).astype(BF16)
            for kh in range(2):
                for c in range(2):
                    at = kh * 64 + c * 32
                    outs[2 * kh + kl][pl.ds(c * HALF + z * 32, 32), :] = piece[at : at + 32]
    same = eye()
    for b in range(KV // 128):
        piece = dot(same, grad_ref[:, b * 128 : (b + 1) * 128], NT).astype(BF16)
        for out in outs:
            out[pl.ds(SLICE + b * 128, 128), :] = piece


def scale_rows(codes_ref, scales_ref, copies, codes, scales, sems):
    loads = [
        pltpu.make_async_copy(codes_ref, codes, sems.at[0]),
        pltpu.make_async_copy(scales_ref, scales, sems.at[1]),
    ]
    for load in loads:
        load.start()
    for load in loads:
        load.wait()
    for b in range(KV // BLOCK):
        at = slice(b * BLOCK, (b + 1) * BLOCK)
        scaled = codes[:, at].astype(F32) * scales[:, b : b + 1].astype(F32)
        copies[:, :, at] = jnp.broadcast_to(scaled.astype(BF16)[None], (NZ, ROWS, BLOCK))


def partial_sums(r0, r2, r1, r3, keep, send):
    c = lax.axis_index("c")
    refs = (r0, r1, r2, r3)
    grads = jnp.concatenate([r[SLICE:, :] for r in refs], axis=1)
    for out, half in ((send, 1 - c), (keep, c)):
        at = pl.ds(pl.multiple_of(half * HALF, HALF), HALF)
        rows = jnp.concatenate([r[at, :] for r in refs], axis=1)
        out[...] = dot(rows, grads, NT).astype(BF16)


def add_cores(a, b, out):
    total = (a[...].astype(F32) + b[...].astype(F32)).astype(BF16)
    out[...] = dot(y_outer(), total, NN).astype(BF16)


def sum_over_y(blocks, out):
    total = jnp.sum(blocks[...].astype(F32), axis=0)
    for z in range(NZ):
        out[z] = total[z * ROWS : (z + 1) * ROWS].astype(BF16)


def apply_weight(own, other, r0, r1, r2, r3, o0, o1, o2, o3, weight):
    c = lax.axis_index("c")
    refs, outs = (r0, r1, r2, r3), (o0, o1, o2, o3)
    order = y_outer()
    for ref, half in ((own, c), (other, 1 - c)):
        at = pl.ds(pl.multiple_of(half * HALF, HALF), HALF)
        weight[at, :] = dot(order, ref[...], TN).astype(BF16)
    w = weight[...]
    grads = jnp.concatenate([r[SLICE:, :] for r in refs], axis=1)
    back = dot(w, grads, NN).astype(BF16)
    for k, out in enumerate(outs):
        out[:SLICE, :] = back[:, k * TOK : (k + 1) * TOK]
    rows = jnp.concatenate([r[:SLICE, :] for r in refs], axis=1)
    keys = dot(w, rows, TN).astype(BF16)
    for k, out in enumerate(outs):
        out[SLICE:, :] = keys[:, k * TOK : (k + 1) * TOK]


def finish(f0, f2, f1, f3, keys, input_grad):
    xh, xl = lax.axis_index("xh"), lax.axis_index("xl")
    refs = (f0, f1, f2, f3)
    same, split = eye(), x_split(xh)
    for b in range(KV // 128):
        at = pl.ds(SLICE + b * 128, 128)
        total = sum(r[at, :].astype(F32) for r in refs).astype(BF16)
        keys[:, b * 128 : (b + 1) * 128] = dot(total, same, TN).astype(BF16)
    for kl in range(2):
        col = (xl if kl == 0 else 1 - xl) * (NZ * 128)
        for z in range(NZ):
            piece = jnp.concatenate(
                [
                    refs[2 * kh + kl][pl.ds(c * HALF + z * 32, 32), :]
                    for kh in range(2)
                    for c in range(2)
                ],
                axis=0,
            )
            block = dot(piece, split, TN).astype(BF16)
            input_grad[:, pl.ds(pl.multiple_of(col + z * 128, 128), 128)] = block


def kernel(body, outs, flops, moved, scratch=(), in_hbm=0, vmem=24):
    pinned = [pl.BlockSpec(memory_space=pl.ANY)] * in_hbm
    return pl.pallas_call(
        body,
        **({"in_specs": pinned} if in_hbm else {}),
        out_shape=[jax.ShapeDtypeStruct(s, BF16) for s in outs],
        scratch_shapes=list(scratch),
        compiler_params=pltpu.CompilerParams(vmem_limit_bytes=vmem << 20),
        cost_estimate=pl.CostEstimate(flops=flops, bytes_accessed=moved, transcendentals=0),
        interpret=INTERPRET,
    )


def exchange(blocks, axis):
    return lax.all_to_all(blocks, axis, split_axis=0, concat_axis=0, tiled=True)


def far_first(blocks):
    return [blocks[k] for k in (0, 2, 1, 3)]


def to_members(blocks):
    return (
        blocks[0],
        lax.ppermute(blocks[1], "xl", SWAP),
        lax.ppermute(blocks[2], "xh", SWAP),
        lax.ppermute(blocks[3], ("xh", "xl"), [(0, 3), (1, 2), (2, 1), (3, 0)]),
    )


def shards(tokens, key_grad, codes, scales):
    room = [
        pltpu.VMEM((ROWS, KV), BF16),
        pltpu.VMEM((ROWS, KV // BLOCK), BF16),
        pltpu.SemaphoreType.DMA((2,)),
    ]
    (copies,) = kernel(scale_rows, [(NZ, ROWS, KV)], 1 << 12, 1 << 17, room, 2, 60)(codes, scales)
    blocks = kernel(prepare, [(PAY, TOK)] * 4, 1 << 28, 3 << 20)(tokens, key_grad)
    work = to_members(blocks)
    by_z = exchange(copies, "z")
    by_z = by_z.reshape(NZ * ROWS, KV)
    by_y = exchange(jnp.broadcast_to(by_z[None], (NY, NZ * ROWS, KV)), "y")
    keep, send = kernel(partial_sums, [(HALF, KV)] * 2, 1 << 29, 3 << 20)(*far_first(work))
    got = lax.ppermute(send, "c", SWAP)
    (total,) = kernel(add_cores, [(HALF, KV)], 1 << 28, 3 << 19)(keep, got)
    by_y, total = lax.optimization_barrier((by_y, total))
    own = by_y.reshape(HALF, KV)
    other = lax.ppermute(own, "c", SWAP)
    total = exchange(total.reshape(NY, NZ * ROWS, KV), "y")
    (total,) = kernel(sum_over_y, [(NZ, ROWS, KV)], 1 << 18, 1 << 20)(total)
    total = exchange(total, "z")
    results = kernel(
        apply_weight, [(PAY, TOK)] * 4, 1 << 30, 4 << 20, [pltpu.VMEM((SLICE, KV), BF16)]
    )(own, other, *work)
    results = to_members(results)
    total, mine = lax.optimization_barrier((total, results[0]))
    results = (mine, *results[1:])
    weight_grad = jnp.sum(total.astype(F32), axis=0)
    d_in = 4 * SLICE
    keys, input_grad = kernel(finish, [(TOK, KV), (TOK, d_in)], 1 << 28, 3 << 20)(
        *far_first(results)
    )
    return keys, input_grad, weight_grad


def solution(mesh):
    torus = Mesh(mesh.devices.reshape(2, NY, 2, NZ, 2), ("xh", "y", "xl", "z", "c"))
    tokens_over = P(INTER + INTRA, None)
    rows_over = P(INTRA + INTER, None)
    return jax.shard_map(
        shards,
        mesh=torus,
        in_specs=(tokens_over, tokens_over, rows_over, rows_over),
        out_specs=(tokens_over, tokens_over, rows_over),
        check_vma=False,
    )
```

```python
import jax
import jax.numpy as jnp
from jax import lax
from jax.experimental import pallas as pl
from jax.experimental.pallas import tpu as pltpu
from jax.sharding import Mesh, PartitionSpec as P

KV = 512
BLOCK = 128
TOK = 128
NY = 8
NZ = 16
ROWS = 4
HALF = NZ * NY * ROWS
SLICE = 2 * HALF
PAY = SLICE + KV
INTER = ("xh", "y")
INTRA = ("xl", "z", "c")
F32 = jnp.float32
BF16 = jnp.bfloat16
INTERPRET = False
SWAP = [(0, 1), (1, 0)]
NN = (((1,), (0,)), ((), ()))
NT = (((1,), (1,)), ((), ()))
TN = (((0,), (0,)), ((), ()))


def dot(a, b, dims):
    return lax.dot_general(a, b, dims, preferred_element_type=F32)


def iota(shape, dim):
    return lax.broadcasted_iota(jnp.int32, shape, dim)


def one_hot(hit):
    return jnp.where(hit, 1.0, 0.0).astype(BF16)


def x_split(xh):
    row, lane = iota((128, 128), 0), iota((128, 128), 1)
    c, q = (row >> 5) & 1, row & 31
    half = jnp.where(row < 64, xh, 1 - xh)
    return one_hot(lane == c * 64 + half * 32 + q)


def y_outer():
    row, col = iota((HALF, HALF), 0), iota((HALF, HALF), 1)
    r = row & (ROWS - 1)
    z = (row >> 2) & (NZ - 1)
    y = row // (NZ * ROWS)
    return one_hot(col == z * (NY * ROWS) + y * ROWS + r)


def eye():
    return one_hot(iota((128, 128), 0) == iota((128, 128), 1))


def prepare(tok_ref, grad_ref, *outs):
    xh, xl = lax.axis_index("xh"), lax.axis_index("xl")
    split = x_split(xh)
    for kl in range(2):
        col = (xl if kl == 0 else 1 - xl) * (NZ * 128)
        for z in range(NZ):
            block = tok_ref[:, pl.ds(pl.multiple_of(col + z * 128, 128), 128)]
            piece = dot(split, block, NT).astype(BF16)
            for kh in range(2):
                for c in range(2):
                    at = kh * 64 + c * 32
                    outs[2 * kh + kl][pl.ds(c * HALF + z * 32, 32), :] = piece[at : at + 32]
    same = eye()
    for b in range(KV // 128):
        piece = dot(same, grad_ref[:, b * 128 : (b + 1) * 128], NT).astype(BF16)
        for out in outs:
            out[pl.ds(SLICE + b * 128, 128), :] = piece


def scale_rows(codes_ref, scales_ref, tok_ref, copies, codes, scales, sems):
    del tok_ref
    loads = [
        pltpu.make_async_copy(codes_ref, codes, sems.at[0]),
        pltpu.make_async_copy(scales_ref, scales, sems.at[1]),
    ]
    for load in loads:
        load.start()
    for load in loads:
        load.wait()
    for b in range(KV // BLOCK):
        at = slice(b * BLOCK, (b + 1) * BLOCK)
        scaled = codes[:, at].astype(F32) * scales[:, b : b + 1].astype(F32)
        copies[:, :, at] = jnp.broadcast_to(scaled.astype(BF16)[None], (NZ, ROWS, BLOCK))


def partial_sums(r0, r2, r1, r3, keep, send):
    c = lax.axis_index("c")
    refs = (r0, r1, r2, r3)
    grads = jnp.concatenate([r[SLICE:, :] for r in refs], axis=1)
    for out, half in ((send, 1 - c), (keep, c)):
        at = pl.ds(pl.multiple_of(half * HALF, HALF), HALF)
        rows = jnp.concatenate([r[at, :] for r in refs], axis=1)
        out[...] = dot(rows, grads, NT).astype(BF16)


def add_cores(a, b, out):
    total = (a[...].astype(F32) + b[...].astype(F32)).astype(BF16)
    out[...] = dot(y_outer(), total, NN).astype(BF16)


def sum_over_y(blocks, out):
    total = jnp.sum(blocks[...].astype(F32), axis=0)
    for z in range(NZ):
        out[z] = total[z * ROWS : (z + 1) * ROWS].astype(BF16)


def apply_weight(own, other, r0, r1, r2, r3, o0, o1, o2, o3, weight):
    c = lax.axis_index("c")
    refs, outs = (r0, r1, r2, r3), (o0, o1, o2, o3)
    order = y_outer()
    for ref, half in ((own, c), (other, 1 - c)):
        at = pl.ds(pl.multiple_of(half * HALF, HALF), HALF)
        weight[at, :] = dot(order, ref[...], TN).astype(BF16)
    w = weight[...]
    grads = jnp.concatenate([r[SLICE:, :] for r in refs], axis=1)
    back = dot(w, grads, NN).astype(BF16)
    for k, out in enumerate(outs):
        out[:SLICE, :] = back[:, k * TOK : (k + 1) * TOK]
    rows = jnp.concatenate([r[:SLICE, :] for r in refs], axis=1)
    keys = dot(w, rows, TN).astype(BF16)
    for k, out in enumerate(outs):
        out[SLICE:, :] = keys[:, k * TOK : (k + 1) * TOK]


def finish(f0, f2, f1, f3, sums, keys, input_grad, weight_grad):
    xh, xl = lax.axis_index("xh"), lax.axis_index("xl")
    weight_grad[...] = jnp.sum(sums[...].astype(F32), axis=0)
    refs = (f0, f1, f2, f3)
    same, split = eye(), x_split(xh)
    for b in range(KV // 128):
        at = pl.ds(SLICE + b * 128, 128)
        total = sum(r[at, :].astype(F32) for r in refs).astype(BF16)
        keys[:, b * 128 : (b + 1) * 128] = dot(total, same, TN).astype(BF16)
    for kl in range(2):
        col = (xl if kl == 0 else 1 - xl) * (NZ * 128)
        for z in range(NZ):
            piece = jnp.concatenate(
                [
                    refs[2 * kh + kl][pl.ds(c * HALF + z * 32, 32), :]
                    for kh in range(2)
                    for c in range(2)
                ],
                axis=0,
            )
            block = dot(piece, split, TN).astype(BF16)
            input_grad[:, pl.ds(pl.multiple_of(col + z * 128, 128), 128)] = block


def kernel(body, outs, flops, moved, scratch=(), in_hbm=0, vmem=24, last=BF16):
    pinned = [pl.BlockSpec(memory_space=pl.ANY)] * in_hbm
    return pl.pallas_call(
        body,
        **({"in_specs": pinned} if in_hbm else {}),
        out_shape=[
            *(jax.ShapeDtypeStruct(s, BF16) for s in outs[:-1]),
            jax.ShapeDtypeStruct(outs[-1], last),
        ],
        scratch_shapes=list(scratch),
        compiler_params=pltpu.CompilerParams(vmem_limit_bytes=vmem << 20),
        cost_estimate=pl.CostEstimate(flops=flops, bytes_accessed=moved, transcendentals=0),
        interpret=INTERPRET,
    )


def exchange(blocks, axis):
    return lax.all_to_all(blocks, axis, split_axis=0, concat_axis=0, tiled=True)


def far_first(blocks):
    return [blocks[k] for k in (0, 2, 1, 3)]


def to_members(blocks):
    return (
        blocks[0],
        lax.ppermute(blocks[1], "xl", SWAP),
        lax.ppermute(blocks[2], "xh", SWAP),
        lax.ppermute(blocks[3], ("xh", "xl"), [(0, 3), (1, 2), (2, 1), (3, 0)]),
    )


def shards(tokens, key_grad, codes, scales):
    room = [
        pltpu.VMEM((ROWS, KV), BF16),
        pltpu.VMEM((ROWS, KV // BLOCK), BF16),
        pltpu.SemaphoreType.DMA((2,)),
    ]
    (copies,) = kernel(scale_rows, [(NZ, ROWS, KV)], 1 << 12, 1 << 17, room, 3, 60)(codes, scales, tokens)
    blocks = kernel(prepare, [(PAY, TOK)] * 4, 1 << 28, 3 << 20)(tokens, key_grad)
    work = to_members(blocks)
    by_z = exchange(copies, "z")
    by_z = by_z.reshape(NZ * ROWS, KV)
    by_y = exchange(jnp.broadcast_to(by_z[None], (NY, NZ * ROWS, KV)), "y")
    keep, send = kernel(partial_sums, [(HALF, KV)] * 2, 1 << 29, 3 << 20)(*far_first(work))
    got = lax.ppermute(send, "c", SWAP)
    (total,) = kernel(add_cores, [(HALF, KV)], 1 << 28, 3 << 19)(keep, got)
    by_y, total = lax.optimization_barrier((by_y, total))
    own = by_y.reshape(HALF, KV)
    other = lax.ppermute(own, "c", SWAP)
    total = exchange(total.reshape(NY, NZ * ROWS, KV), "y")
    (total,) = kernel(sum_over_y, [(NZ, ROWS, KV)], 1 << 18, 1 << 20)(total)
    total = exchange(total, "z")
    results = kernel(
        apply_weight, [(PAY, TOK)] * 4, 1 << 33, 4 << 20, [pltpu.VMEM((SLICE, KV), BF16)]
    )(own, other, *work)
    results = to_members(results)
    total, mine = lax.optimization_barrier((total, results[0]))
    results = (mine, *results[1:])
    shapes = [(TOK, KV), (TOK, 4 * SLICE), (ROWS, KV)]
    keys, input_grad, weight_grad = kernel(finish, shapes, 1 << 28, 3 << 20, last=F32)(
        *far_first(results), total
    )
    return keys, input_grad, weight_grad


def solution(mesh):
    torus = Mesh(mesh.devices.reshape(2, NY, 2, NZ, 2), ("xh", "y", "xl", "z", "c"))
    tokens_over = P(INTER + INTRA, None)
    rows_over = P(INTRA + INTER, None)
    return jax.shard_map(
        shards,
        mesh=torus,
        in_specs=(tokens_over, tokens_over, rows_over, rows_over),
        out_specs=(tokens_over, tokens_over, rows_over),
        check_vma=False,
    )
```

```python
import jax
import jax.numpy as jnp
from jax import lax
from jax.experimental import pallas as pl
from jax.experimental.pallas import tpu as pltpu
from jax.sharding import Mesh, PartitionSpec as P

KV = 512
BLOCK = 128
TOK = 128
NY = 8
NZ = 16
ROWS = 4
HALF = NZ * NY * ROWS
SLICE = 2 * HALF
PAY = SLICE + KV
INTER = ("xh", "y")
INTRA = ("xl", "z", "c")
F32 = jnp.float32
BF16 = jnp.bfloat16
INTERPRET = False
SWAP = [(0, 1), (1, 0)]
NN = (((1,), (0,)), ((), ()))
NT = (((1,), (1,)), ((), ()))
TN = (((0,), (0,)), ((), ()))


def dot(a, b, dims):
    return lax.dot_general(a, b, dims, preferred_element_type=F32)


def iota(shape, dim):
    return lax.broadcasted_iota(jnp.int32, shape, dim)


def one_hot(hit):
    return jnp.where(hit, 1.0, 0.0).astype(BF16)


def x_split(xh):
    row, lane = iota((128, 128), 0), iota((128, 128), 1)
    c, q = (row >> 5) & 1, row & 31
    half = jnp.where(row < 64, xh, 1 - xh)
    return one_hot(lane == c * 64 + half * 32 + q)


def y_outer():
    row, col = iota((HALF, HALF), 0), iota((HALF, HALF), 1)
    r = row & (ROWS - 1)
    z = (row >> 2) & (NZ - 1)
    y = row // (NZ * ROWS)
    return one_hot(col == z * (NY * ROWS) + y * ROWS + r)


def eye():
    return one_hot(iota((128, 128), 0) == iota((128, 128), 1))


def prepare(tok_ref, grad_ref, *outs):
    xh, xl = lax.axis_index("xh"), lax.axis_index("xl")
    split = x_split(xh)
    for kl in range(2):
        col = (xl if kl == 0 else 1 - xl) * (NZ * 128)
        for z in range(NZ):
            block = tok_ref[:, pl.ds(pl.multiple_of(col + z * 128, 128), 128)]
            piece = dot(split, block, NT).astype(BF16)
            for kh in range(2):
                for c in range(2):
                    at = kh * 64 + c * 32
                    outs[2 * kh + kl][pl.ds(c * HALF + z * 32, 32), :] = piece[at : at + 32]
    same = eye()
    for b in range(KV // 128):
        piece = dot(same, grad_ref[:, b * 128 : (b + 1) * 128], NT).astype(BF16)
        for out in outs:
            out[pl.ds(SLICE + b * 128, 128), :] = piece


def scale_rows(codes_ref, scales_ref, tok_ref, copies, codes, scales, sems):
    del tok_ref
    loads = [
        pltpu.make_async_copy(codes_ref, codes, sems.at[0]),
        pltpu.make_async_copy(scales_ref, scales, sems.at[1]),
    ]
    for load in loads:
        load.start()
    for load in loads:
        load.wait()
    for b in range(KV // BLOCK):
        at = slice(b * BLOCK, (b + 1) * BLOCK)
        scaled = codes[:, at].astype(F32) * scales[:, b : b + 1].astype(F32)
        copies[:, :, at] = jnp.broadcast_to(scaled.astype(BF16)[None], (NZ, ROWS, BLOCK))


def spread(blocks, copies, rows):
    for z in range(NZ):
        rows[z * ROWS : (z + 1) * ROWS, :] = blocks[z].astype(F32)
    same = rows[...].astype(BF16)
    for y in range(NY):
        copies[y] = same


def partial_sums(r0, r2, r1, r3, keep, send):
    c = lax.axis_index("c")
    refs = (r0, r1, r2, r3)
    grads = jnp.concatenate([r[SLICE:, :] for r in refs], axis=1)
    for out, half in ((send, 1 - c), (keep, c)):
        at = pl.ds(pl.multiple_of(half * HALF, HALF), HALF)
        rows = jnp.concatenate([r[at, :] for r in refs], axis=1)
        out[...] = dot(rows, grads, NT).astype(BF16)


def add_cores(a, b, out):
    total = (a[...].astype(F32) + b[...].astype(F32)).astype(BF16)
    out[...] = dot(y_outer(), total, NN).astype(BF16)


def sum_over_y(blocks, out):
    total = jnp.sum(blocks[...].astype(F32), axis=0)
    for z in range(NZ):
        out[z] = total[z * ROWS : (z + 1) * ROWS].astype(BF16)


def apply_weight(own, other, r0, r1, r2, r3, o0, o1, o2, o3, weight):
    c = lax.axis_index("c")
    refs, outs = (r0, r1, r2, r3), (o0, o1, o2, o3)
    order = y_outer()
    for ref, half in ((own, c), (other, 1 - c)):
        at = pl.ds(pl.multiple_of(half * HALF, HALF), HALF)
        weight[at, :] = dot(order, ref[...], TN).astype(BF16)
    w = weight[...]
    grads = jnp.concatenate([r[SLICE:, :] for r in refs], axis=1)
    back = dot(w, grads, NN).astype(BF16)
    for k, out in enumerate(outs):
        out[:SLICE, :] = back[:, k * TOK : (k + 1) * TOK]
    rows = jnp.concatenate([r[:SLICE, :] for r in refs], axis=1)
    keys = dot(w, rows, TN).astype(BF16)
    for k, out in enumerate(outs):
        out[SLICE:, :] = keys[:, k * TOK : (k + 1) * TOK]


def finish(f0, f2, f1, f3, sums, keys, input_grad, weight_grad):
    xh, xl = lax.axis_index("xh"), lax.axis_index("xl")
    weight_grad[...] = jnp.sum(sums[...].astype(F32), axis=0)
    refs = (f0, f1, f2, f3)
    same, split = eye(), x_split(xh)
    for b in range(KV // 128):
        at = pl.ds(SLICE + b * 128, 128)
        total = sum(r[at, :].astype(F32) for r in refs).astype(BF16)
        keys[:, b * 128 : (b + 1) * 128] = dot(total, same, TN).astype(BF16)
    for kl in range(2):
        col = (xl if kl == 0 else 1 - xl) * (NZ * 128)
        for z in range(NZ):
            piece = jnp.concatenate(
                [
                    refs[2 * kh + kl][pl.ds(c * HALF + z * 32, 32), :]
                    for kh in range(2)
                    for c in range(2)
                ],
                axis=0,
            )
            block = dot(piece, split, TN).astype(BF16)
            input_grad[:, pl.ds(pl.multiple_of(col + z * 128, 128), 128)] = block


def kernel(body, outs, flops, moved, scratch=(), in_hbm=0, vmem=24, last=BF16):
    pinned = [pl.BlockSpec(memory_space=pl.ANY)] * in_hbm
    return pl.pallas_call(
        body,
        **({"in_specs": pinned} if in_hbm else {}),
        out_shape=[
            *(jax.ShapeDtypeStruct(s, BF16) for s in outs[:-1]),
            jax.ShapeDtypeStruct(outs[-1], last),
        ],
        scratch_shapes=list(scratch),
        compiler_params=pltpu.CompilerParams(vmem_limit_bytes=vmem << 20),
        cost_estimate=pl.CostEstimate(flops=flops, bytes_accessed=moved, transcendentals=0),
        interpret=INTERPRET,
    )


def exchange(blocks, axis):
    return lax.all_to_all(blocks, axis, split_axis=0, concat_axis=0, tiled=True)


def far_first(blocks):
    return [blocks[k] for k in (0, 2, 1, 3)]


def to_members(blocks):
    return (
        blocks[0],
        lax.ppermute(blocks[1], "xl", SWAP),
        lax.ppermute(blocks[2], "xh", SWAP),
        lax.ppermute(blocks[3], ("xh", "xl"), [(0, 3), (1, 2), (2, 1), (3, 0)]),
    )


def shards(tokens, key_grad, codes, scales):
    room = [
        pltpu.VMEM((ROWS, KV), BF16),
        pltpu.VMEM((ROWS, KV // BLOCK), BF16),
        pltpu.SemaphoreType.DMA((2,)),
    ]
    (copies,) = kernel(scale_rows, [(NZ, ROWS, KV)], 1 << 12, 1 << 17, room, 3, 60)(codes, scales, tokens)
    blocks = kernel(prepare, [(PAY, TOK)] * 4, 1 << 28, 3 << 20)(tokens, key_grad)
    work = to_members(blocks)
    by_z = exchange(copies, "z")
    (by_z,) = kernel(
        spread,
        [(NY, NZ * ROWS, KV)],
        1 << 18,
        1 << 19,
        [pltpu.VMEM((NZ * ROWS, KV), F32)],
    )(by_z)
    by_y = exchange(by_z, "y")
    keep, send = kernel(partial_sums, [(HALF, KV)] * 2, 1 << 29, 3 << 20)(*far_first(work))
    got = lax.ppermute(send, "c", SWAP)
    (total,) = kernel(add_cores, [(HALF, KV)], 1 << 28, 3 << 19)(keep, got)
    by_y, total = lax.optimization_barrier((by_y, total))
    own = by_y.reshape(HALF, KV)
    other = lax.ppermute(own, "c", SWAP)
    total = exchange(total.reshape(NY, NZ * ROWS, KV), "y")
    (total,) = kernel(sum_over_y, [(NZ, ROWS, KV)], 1 << 18, 1 << 20)(total)
    total = exchange(total, "z")
    results = kernel(
        apply_weight, [(PAY, TOK)] * 4, 1 << 33, 4 << 20, [pltpu.VMEM((SLICE, KV), BF16)]
    )(own, other, *work)
    results = to_members(results)
    total, mine = lax.optimization_barrier((total, results[0]))
    results = (mine, *results[1:])
    shapes = [(TOK, KV), (TOK, 4 * SLICE), (ROWS, KV)]
    keys, input_grad, weight_grad = kernel(finish, shapes, 1 << 28, 3 << 20, last=F32)(
        *far_first(results), total
    )
    return keys, input_grad, weight_grad


def solution(mesh):
    torus = Mesh(mesh.devices.reshape(2, NY, 2, NZ, 2), ("xh", "y", "xl", "z", "c"))
    tokens_over = P(INTER + INTRA, None)
    rows_over = P(INTRA + INTER, None)
    return jax.shard_map(
        shards,
        mesh=torus,
        in_specs=(tokens_over, tokens_over, rows_over, rows_over),
        out_specs=(tokens_over, tokens_over, rows_over),
        check_vma=False,
    )
```

```python
import jax
import jax.numpy as jnp
from jax import lax
from jax.experimental import pallas as pl
from jax.experimental.pallas import tpu as pltpu
from jax.sharding import Mesh, PartitionSpec as P

KV = 512
BLOCK = 128
TOK = 128
NY = 8
NZ = 16
ROWS = 4
HALF = NZ * NY * ROWS
SLICE = 2 * HALF
PAY = SLICE + KV
INTER = ("xh", "y")
INTRA = ("xl", "z", "c")
F32 = jnp.float32
BF16 = jnp.bfloat16
INTERPRET = False
SWAP = [(0, 1), (1, 0)]
NN = (((1,), (0,)), ((), ()))
NT = (((1,), (1,)), ((), ()))
TN = (((0,), (0,)), ((), ()))


def dot(a, b, dims):
    return lax.dot_general(a, b, dims, preferred_element_type=F32)


def iota(shape, dim):
    return lax.broadcasted_iota(jnp.int32, shape, dim)


def one_hot(hit):
    return jnp.where(hit, 1.0, 0.0).astype(BF16)


def x_split(xh):
    row, lane = iota((128, 128), 0), iota((128, 128), 1)
    c, q = (row >> 5) & 1, row & 31
    half = jnp.where(row < 64, xh, 1 - xh)
    return one_hot(lane == c * 64 + half * 32 + q)


def y_outer():
    row, col = iota((HALF, HALF), 0), iota((HALF, HALF), 1)
    r = row & (ROWS - 1)
    z = (row >> 2) & (NZ - 1)
    y = row // (NZ * ROWS)
    return one_hot(col == z * (NY * ROWS) + y * ROWS + r)


def eye():
    return one_hot(iota((128, 128), 0) == iota((128, 128), 1))


def prepare(tok_ref, grad_ref, *outs):
    xh, xl = lax.axis_index("xh"), lax.axis_index("xl")
    split = x_split(xh)
    for kl in range(2):
        col = (xl if kl == 0 else 1 - xl) * (NZ * 128)
        for z in range(NZ):
            block = tok_ref[:, pl.ds(pl.multiple_of(col + z * 128, 128), 128)]
            piece = dot(split, block, NT).astype(BF16)
            for kh in range(2):
                for c in range(2):
                    at = kh * 64 + c * 32
                    outs[2 * kh + kl][pl.ds(c * HALF + z * 32, 32), :] = piece[at : at + 32]
    same = eye()
    for b in range(KV // 128):
        piece = dot(same, grad_ref[:, b * 128 : (b + 1) * 128], NT).astype(BF16)
        for out in outs:
            out[pl.ds(SLICE + b * 128, 128), :] = piece


def scale_rows(codes_ref, scales_ref, tok_ref, copies, codes, scales, sems):
    del tok_ref
    loads = [
        pltpu.make_async_copy(codes_ref, codes, sems.at[0]),
        pltpu.make_async_copy(scales_ref, scales, sems.at[1]),
    ]
    for load in loads:
        load.start()
    for load in loads:
        load.wait()
    for b in range(KV // BLOCK):
        at = slice(b * BLOCK, (b + 1) * BLOCK)
        scaled = codes[:, at].astype(F32) * scales[:, b : b + 1].astype(F32)
        copies[:, :, at] = jnp.broadcast_to(scaled.astype(BF16)[None], (NZ, ROWS, BLOCK))


def spread(blocks, copies, rows):
    for z in range(NZ):
        rows[z * ROWS : (z + 1) * ROWS, :] = blocks[z].astype(F32)
    same = rows[...].astype(BF16)
    for y in range(NY):
        copies[y] = same


def partial_sums(r0, r2, r1, r3, keep, send):
    c = lax.axis_index("c")
    refs = (r0, r1, r2, r3)
    grads = jnp.concatenate([r[SLICE:, :] for r in refs], axis=1)
    for out, half in ((send, 1 - c), (keep, c)):
        at = pl.ds(pl.multiple_of(half * HALF, HALF), HALF)
        rows = jnp.concatenate([r[at, :] for r in refs], axis=1)
        out[...] = dot(rows, grads, NT).astype(BF16)


def add_cores(a, b, out):
    total = (a[...].astype(F32) + b[...].astype(F32)).astype(BF16)
    out[...] = dot(y_outer(), total, NN).astype(BF16)


def sum_over_y(blocks, out):
    total = jnp.sum(blocks[...].astype(F32), axis=0)
    for z in range(NZ):
        out[z] = total[z * ROWS : (z + 1) * ROWS].astype(BF16)


def apply_weight(own, other, r0, r1, r2, r3, o0, o1, o2, o3, weight):
    c = lax.axis_index("c")
    refs, outs = (r0, r1, r2, r3), (o0, o1, o2, o3)
    order = y_outer()
    for ref, half in ((own, c), (other, 1 - c)):
        at = pl.ds(pl.multiple_of(half * HALF, HALF), HALF)
        weight[at, :] = dot(order, ref[...], TN).astype(BF16)
    w = weight[...]
    grads = jnp.concatenate([r[SLICE:, :] for r in refs], axis=1)
    back = dot(w, grads, NN).astype(BF16)
    for k, out in enumerate(outs):
        out[:SLICE, :] = back[:, k * TOK : (k + 1) * TOK]
    rows = jnp.concatenate([r[:SLICE, :] for r in refs], axis=1)
    keys = dot(w, rows, TN).astype(BF16)
    for k, out in enumerate(outs):
        out[SLICE:, :] = keys[:, k * TOK : (k + 1) * TOK]


def finish(f0, f2, f1, f3, sums, keys, input_grad, weight_grad):
    xh, xl = lax.axis_index("xh"), lax.axis_index("xl")
    weight_grad[...] = jnp.sum(sums[...].astype(F32), axis=0)
    refs = (f0, f1, f2, f3)
    same, split = eye(), x_split(xh)
    for b in range(KV // 128):
        at = pl.ds(SLICE + b * 128, 128)
        total = sum(r[at, :].astype(F32) for r in refs).astype(BF16)
        keys[:, b * 128 : (b + 1) * 128] = dot(total, same, TN).astype(BF16)
    for kl in range(2):
        col = (xl if kl == 0 else 1 - xl) * (NZ * 128)
        for z in range(NZ):
            piece = jnp.concatenate(
                [
                    refs[2 * kh + kl][pl.ds(c * HALF + z * 32, 32), :]
                    for kh in range(2)
                    for c in range(2)
                ],
                axis=0,
            )
            block = dot(piece, split, TN).astype(BF16)
            input_grad[:, pl.ds(pl.multiple_of(col + z * 128, 128), 128)] = block


def kernel(body, outs, flops, moved, scratch=(), in_hbm=0, vmem=24, last=BF16):
    pinned = [pl.BlockSpec(memory_space=pl.ANY)] * in_hbm
    return pl.pallas_call(
        body,
        **({"in_specs": pinned} if in_hbm else {}),
        out_shape=[
            *(jax.ShapeDtypeStruct(s, BF16) for s in outs[:-1]),
            jax.ShapeDtypeStruct(outs[-1], last),
        ],
        scratch_shapes=list(scratch),
        compiler_params=pltpu.CompilerParams(vmem_limit_bytes=vmem << 20),
        cost_estimate=pl.CostEstimate(flops=flops, bytes_accessed=moved, transcendentals=0),
        interpret=INTERPRET,
    )


def exchange(blocks, axis):
    return lax.all_to_all(blocks, axis, split_axis=0, concat_axis=0, tiled=True)


def far_first(blocks):
    return [blocks[k] for k in (0, 2, 1, 3)]


def to_members(blocks):
    return (
        blocks[0],
        lax.ppermute(blocks[1], "xl", SWAP),
        lax.ppermute(blocks[2], "xh", SWAP),
        lax.ppermute(blocks[3], ("xh", "xl"), [(0, 3), (1, 2), (2, 1), (3, 0)]),
    )


def shards(tokens, key_grad, codes, scales):
    room = [
        pltpu.VMEM((ROWS, KV), BF16),
        pltpu.VMEM((ROWS, KV // BLOCK), BF16),
        pltpu.SemaphoreType.DMA((2,)),
    ]
    (copies,) = kernel(scale_rows, [(NZ, ROWS, KV)], 1 << 12, 1 << 17, room, 3, 60)(codes, scales, tokens)
    blocks = kernel(prepare, [(PAY, TOK)] * 4, 1 << 28, 3 << 20)(tokens, key_grad)
    work = to_members(blocks)
    by_z = exchange(copies, "z")
    (by_z,) = kernel(
        spread,
        [(NY, NZ * ROWS, KV)],
        1 << 18,
        1 << 19,
        [pltpu.VMEM((NZ * ROWS, KV), F32)],
    )(by_z)
    by_y = exchange(by_z, "y")
    keep, send = kernel(partial_sums, [(HALF, KV)] * 2, 1 << 29, 3 << 20)(*far_first(work))
    got = lax.ppermute(send, "c", SWAP)
    (total,) = kernel(add_cores, [(HALF, KV)], 1 << 28, 3 << 19)(keep, got)
    by_y, total = lax.optimization_barrier((by_y, total))
    own = by_y.reshape(HALF, KV)
    other = lax.ppermute(own, "c", SWAP)
    total = exchange(total.reshape(NY, NZ * ROWS, KV), "y")
    (total,) = kernel(sum_over_y, [(NZ, ROWS, KV)], 1 << 18, 1 << 20)(total)
    total = exchange(total, "z")
    results = kernel(
        apply_weight, [(PAY, TOK)] * 4, 1 << 30, 4 << 20, [pltpu.VMEM((SLICE, KV), BF16)]
    )(own, other, *work)
    results = to_members(results)
    total, mine = lax.optimization_barrier((total, results[0]))
    results = (mine, *results[1:])
    shapes = [(TOK, KV), (TOK, 4 * SLICE), (ROWS, KV)]
    keys, input_grad, weight_grad = kernel(finish, shapes, 1 << 28, 3 << 20, last=F32)(
        *far_first(results), total
    )
    return keys, input_grad, weight_grad


def solution(mesh):
    torus = Mesh(mesh.devices.reshape(2, NY, 2, NZ, 2), ("xh", "y", "xl", "z", "c"))
    tokens_over = P(INTER + INTRA, None)
    rows_over = P(INTRA + INTER, None)
    return jax.shard_map(
        shards,
        mesh=torus,
        in_specs=(tokens_over, tokens_over, rows_over, rows_over),
        out_specs=(tokens_over, tokens_over, rows_over),
        check_vma=False,
    )
```
